32 devices in a mesh: groups: 2 (over y), fsdp: 4 (over z), tp: 2 (over x), seq: 2 (over core).
Axes of the slice: x: 2, y: 2, z: 4, core: 2. Of those that a mesh axis runs over, the one named last changes fastest.
Arguments:
- tokens: bfloat16 [12288, 5120], P(('groups', 'fsdp', 'seq'), 'tp'), parts along dimension 0, may hold values from -8 to 8
- doc_ids: int32 [12288], P(('groups', 'fsdp', 'seq')), parts along dimension 0, may hold values from 0 to 23, as said below
- block_dest: int32 [768], P(('groups', 'fsdp', 'seq')), parts along dimension 0, may hold values from 0 to 383, as said below
- norm_gain: float32 [5120], replicated, may hold values from 0.1 to 1.9
- w_query: bfloat16 [5120, 4096], P('fsdp', 'tp'), as said below
- w_key: bfloat16 [5120, 512], P('fsdp', 'tp'), as said below
- w_value: bfloat16 [5120, 512], P('fsdp', 'tp'), may hold values from -0.078125 to 0.078125
- query_gain: float32 [128], replicated, as said below
- key_gain: float32 [128], replicated, as said below
Outputs:
- attended: bfloat16 [12288, 4096], P(('groups', 'fsdp', 'seq'), 'tp'), parts along dimension 0
The draws below stay inside these ranges and needn't reach their ends.
There are 2 independent parts, one for each index of `groups`. The reference program is written for one: setup_inputs(seed, part) draws one part's arguments, and reference() takes and returns one part's arrays. A program takes and returns all parts, laid end to end along the dimension named above; an argument that names none is the same for every part. Nothing has to cross between parts.
Inputs may be any that keep to these rules, and one draw needn't show every extreme that they name: `doc_ids`: trainer device d holds rows d * 768 to (d + 1) * 768 - 1; its ids are d * 3 to d * 3 + 2, in order, each on a run of rows of its own. A permutation of the blocks; owner device d holds blocks d * 48 onward, trainer device of a block is block_dest // 48; each owner device sends at most 6 blocks to one trainer device and exactly 6 to some; the j-th blocks of all owner devices go to different trainer devices. `w_query`: entries of order 5120^-1/2. `w_key`: entries of order 5120^-1/2. `query_gain`: positive gains. `key_gain`: positive gains.
All inputs are finite; a program needn't handle non-finite values.
Results may differ from the reference program's by a relative error of at most 0.0085.
Values may be sent and summed in bfloat16 or wider, within the bound.
A program may use at most 128 MiB of HBM per device.

```python
import math
import jax
import jax.numpy as jnp
from jax import lax

D = 5120
QHEADS = 32
KVHEADS = 4
HEAD_DIM = 128
TOK_DEV = 768
BLOCK = 16
NSEG = 3
TOKENS = 6144
N_FSDP = 4
N_SEQ = 2


def draw_tokens(key, part):
    key = jax.random.fold_in(key, 3)
    values = jax.random.normal(key, (TOKENS, D), jnp.float32)
    return jnp.clip(values, -8.0, 8.0).astype(jnp.bfloat16)


def draw_doc_ids(key, part):
    key = jax.random.fold_in(key, 7)
    device_count = N_FSDP * N_SEQ
    key_list = jax.random.split(key, device_count)

    def device_ids(device_key):
        cut_points = jax.random.permutation(device_key, TOK_DEV - 1)[:NSEG - 1] + 1
        return jnp.sum((cut_points[None, :] <= jnp.arange(TOK_DEV)[:, None]).astype(jnp.int32), axis=1)
    local_ids = jax.vmap(device_ids)(key_list)
    return (local_ids + NSEG * jnp.arange(device_count)[:, None]).reshape(-1).astype(jnp.int32)


def draw_block_dest(key, part):
    key = jax.random.fold_in(key, 11)
    device_count = N_FSDP * N_SEQ
    block_count = TOK_DEV // BLOCK
    repeats = (block_count + device_count - 1) // device_count
    key_list = jax.random.split(key, repeats + 3)
    offsets = jnp.concatenate([jax.random.permutation(key_list[i], device_count) for i in range(repeats)])[:block_count]
    outer_perm = jax.random.permutation(key_list[repeats], device_count)
    inner_perm = jax.random.permutation(key_list[repeats + 1], device_count)
    slot_perms = jax.vmap(lambda slot_key: jax.random.permutation(slot_key, block_count))(jax.random.split(key_list[repeats + 2], device_count))
    source = jnp.arange(device_count)[:, None]
    target = outer_perm[(inner_perm[source] + offsets[None, :]) % device_count]
    slot_index = slot_perms[target, jnp.arange(block_count)[None, :]]
    return (target * block_count + slot_index).reshape(-1).astype(jnp.int32)


def shared_base(key):
    return jax.random.normal(jax.random.fold_in(key, 5), (D, KVHEADS * HEAD_DIM), jnp.float32)


def draw_w_key(key, part):
    base_values = shared_base(key)
    return (jnp.clip(base_values, -4.5, 4.5) / math.sqrt(D)).astype(jnp.bfloat16)


def draw_w_query(key, part):
    key = jax.random.fold_in(key, 17)
    values = jax.random.normal(key, (D, QHEADS * HEAD_DIM), jnp.float32)
    return (jnp.clip(values, -4.5, 4.5) / math.sqrt(D)).astype(jnp.bfloat16)


def draw_query_gain(key, part):
    key = jax.random.fold_in(key, 19)
    return jax.random.uniform(key, (HEAD_DIM,), jnp.float32, 0.5, 1.6)


def draw_key_gain(key, part):
    key = jax.random.fold_in(key, 23)
    return jax.random.uniform(key, (HEAD_DIM,), jnp.float32, 0.5, 1.6)


def level_of(rng, dims, cuts, smallest, largest):
    factor_of, own = 1.0, jax.random.fold_in(rng, 6)
    for dim, blocks in cuts:
        draws = jnp.exp(jax.random.uniform(jax.random.fold_in(own, dim), (blocks,), jnp.float32, smallest / len(cuts), largest / len(cuts)))
        factor_of = factor_of * jnp.repeat(draws, dims[dim] // blocks).reshape([-1 if axis == dim else 1 for axis in range(len(dims))])
    return factor_of


def noise(stream_key, shape, width, most, cuts=(), held_as=jnp.bfloat16):
    level = level_of(stream_key, shape, cuts, -0.22, 0.18) if cuts else 1.0
    result = jax.random.normal(stream_key, shape, jnp.float32) * width * level
    return jnp.minimum(jnp.maximum(result, -most), most).astype(held_as)


def setup_inputs(seed: int = 0, part: int = 0) -> dict:
    seeds = jax.random.split(jax.random.key(seed), 10)
    own_keys = jax.random.split(jax.random.fold_in(seeds[9], part), 10)
    return {
        "tokens": draw_tokens(jax.random.fold_in(jax.random.fold_in(seeds[9], part), 71), part),
        "doc_ids": draw_doc_ids(jax.random.fold_in(jax.random.fold_in(seeds[9], part), 71), part),
        "block_dest": draw_block_dest(jax.random.fold_in(jax.random.fold_in(seeds[9], part), 71), part),
        "norm_gain": jnp.clip(1.0 + 0.18 * jax.random.normal(seeds[3], (D,), jnp.float32), 0.1, 1.9),
        "w_query": draw_w_query(jax.random.fold_in(seeds[9], 71), part),
        "w_key": draw_w_key(jax.random.fold_in(seeds[9], 71), part),
        "w_value": noise(seeds[6], (D, KVHEADS * HEAD_DIM), D ** -0.5, 0.078125, ((0, 4), (1, 2))),
        "query_gain": draw_query_gain(jax.random.fold_in(seeds[9], 71), part),
        "key_gain": draw_key_gain(jax.random.fold_in(seeds[9], 71), part),
    }


EPS = 1e-06
THETA = 1000000.0

def rms_rows(values, scale_gain):
    return values * lax.rsqrt(lax.optimization_barrier(jnp.mean(values * values, axis=-1, keepdims=True)) + EPS) * scale_gain

def rotate(values, position):
    half_dim = HEAD_DIM // 2
    frequency = THETA ** (-jnp.arange(half_dim, dtype=jnp.float32) * 2.0 / HEAD_DIM)
    angles = position.astype(jnp.float32)[:, None] * frequency[None, :]
    cosine = jnp.concatenate([jnp.cos(angles), jnp.cos(angles)], axis=-1)[:, None, :]
    sine_table = jnp.concatenate([jnp.sin(angles), jnp.sin(angles)], axis=-1)[:, None, :]
    first_half = values[..., :half_dim]
    second_half = values[..., half_dim:]
    turned = jnp.concatenate([-second_half, first_half], axis=-1)
    return values * cosine + turned * sine_table

def attend(query_rows, key_rows, value_rows, doc_rows):
    row_total = query_rows.shape[0]
    head_total = query_rows.shape[1]
    group_size = head_total // key_rows.shape[1]
    row_index = jnp.arange(row_total, dtype=jnp.int32)
    allowed = (doc_rows[:, None] == doc_rows[None, :]) & (row_index[None, :] <= row_index[:, None])

    def one_head(head_index):
        key_index = head_index // group_size
        query_head = lax.dynamic_index_in_dim(query_rows, head_index, 1, keepdims=False)
        key_head = lax.dynamic_index_in_dim(key_rows, key_index, 1, keepdims=False)
        value_head = lax.dynamic_index_in_dim(value_rows, key_index, 1, keepdims=False)
        scores = jnp.dot(query_head, key_head.T, preferred_element_type=jnp.float32)
        scores = jnp.where(allowed, scores, -1e+30)
        row_max = lax.optimization_barrier(jnp.max(scores, axis=1, keepdims=True))
        exponent = jnp.where(allowed, jnp.exp(scores - row_max), 0.0)
        weights = (exponent / lax.optimization_barrier(jnp.sum(exponent, axis=1, keepdims=True))).astype(jnp.bfloat16)
        return jnp.dot(weights, value_head, preferred_element_type=jnp.float32).astype(jnp.bfloat16)
    outputs = lax.map(one_head, jnp.arange(head_total, dtype=jnp.int32))
    return jnp.transpose(outputs, (1, 0, 2)).reshape(row_total, head_total * HEAD_DIM)

def device_rows(rows, doc_rows, norm_gain, w_query, w_key, w_value, query_gain, key_gain):
    row_total = rows.shape[0]
    normed = rms_rows(rows.astype(jnp.float32), norm_gain).astype(jnp.bfloat16)
    query_raw = jnp.dot(normed, w_query, preferred_element_type=jnp.float32).reshape(row_total, -1, HEAD_DIM)
    key_raw = jnp.dot(normed, w_key, preferred_element_type=jnp.float32).reshape(row_total, -1, HEAD_DIM)
    value_rows = jnp.dot(normed, w_value, preferred_element_type=jnp.float32).astype(jnp.bfloat16).reshape(row_total, -1, HEAD_DIM)
    position = jnp.arange(row_total, dtype=jnp.int32) - jnp.searchsorted(doc_rows, doc_rows, side='left').astype(jnp.int32)
    query_rows = (rotate(rms_rows(query_raw, query_gain), position) * HEAD_DIM ** (-0.5)).astype(jnp.bfloat16)
    key_rows = rotate(rms_rows(key_raw, key_gain), position).astype(jnp.bfloat16)
    return attend(query_rows, key_rows, value_rows, doc_rows)

def reference(tokens, doc_ids, block_dest, norm_gain, w_query, w_key, w_value, query_gain, key_gain):
    block_total = block_dest.shape[0]
    inverse = jnp.zeros((block_total,), jnp.int32).at[block_dest].set(jnp.arange(block_total, dtype=jnp.int32))
    trainer = tokens.reshape(block_total, BLOCK, D)[inverse].reshape(-1, TOK_DEV, D)
    doc_rows = doc_ids.reshape(-1, TOK_DEV)

    def handle(members):
        return device_rows(members[0], members[1], norm_gain, w_query, w_key, w_value, query_gain, key_gain)
    outputs = lax.map(handle, (trainer, doc_rows))
    out_blocks = outputs.reshape(block_total, BLOCK, QHEADS * HEAD_DIM)
    return out_blocks[block_dest].reshape(-1, QHEADS * HEAD_DIM)
```

```python
import functools

import jax
import jax.numpy as jnp
from jax import lax
from jax.experimental import pallas as pl
from jax.experimental.pallas import tpu as pltpu
from jax.sharding import PartitionSpec as P

HEAD_DIM = 128
BLOCK = 16
GROUP = 8
ROWS = 256
EPS = 1e-06
THETA = 1000000.0
MESH = pl.DeviceIdType.MESH


def kernel(
    sizes, x_ref, wq_ref, wk_ref, wv_ref, ngain_ref, qgain_ref, kgain_ref, cos_ref, sin_ref, bias_ref,
    ret_ref, w_buf, x_buf, s_buf, r_buf, o_buf,
    own_sem, xl_sem, xs_sem, xr_sem, zs_sem, zr_sem, ys_sem, yr_sem, cs_sem, cr_sem,
    dl_sem, ds_sem, dr_sem, bl_sem, bs_sem, br_sem,
):
    n, tps, cores = sizes
    y, z, t, c = (lax.axis_index(a) for a in ("groups", "fsdp", "tp", "seq"))
    chunks, depth, width = w_buf.shape
    shard = depth // n
    quarter = shard // 4
    rows = x_ref.shape[0]
    feat = x_ref.shape[1]
    peers = n * cores
    slab = rows // peers
    half = width // 2
    me = z * cores + c

    own_rows = pl.ds(pl.multiple_of(z * shard, 16), shard)
    own_copies = [
        [
            pltpu.make_async_copy(wk_ref, w_buf.at[0, own_rows, pl.ds(0, half)], own_sem.at[0]),
            pltpu.make_async_copy(wv_ref, w_buf.at[0, own_rows, pl.ds(half, half)], own_sem.at[chunks]),
        ]
    ]
    for j in range(1, chunks):
        own_copies.append(
            [pltpu.make_async_copy(wq_ref.at[:, pl.ds((j - 1) * width, width)], w_buf.at[j, own_rows, :], own_sem.at[j])]
        )
    for copies in own_copies:
        for copy in copies:
            copy.start()
    x_local = pltpu.make_async_copy(x_ref, x_buf.at[t], xl_sem)
    x_local.start()

    barrier = pltpu.get_barrier_semaphore()

    def peer_of(k):
        p = lax.rem(me + k, peers)
        return p, {"fsdp": p // cores, "seq": lax.rem(p, cores)}

    @pl.loop(1, peers)
    def _(k):
        _, dev = peer_of(k)
        pl.semaphore_signal(barrier, inc=1, device_id=dev, device_id_type=MESH)

    for k in range(1, tps):
        pl.semaphore_signal(barrier, inc=1, device_id={"tp": lax.rem(t + k, tps)}, device_id_type=MESH)
    pl.semaphore_signal(barrier, inc=1, device_id={"groups": 1 - y}, device_id_type=MESH)
    pl.semaphore_wait(barrier, peers - 1 + tps - 1 + 1)

    x_copies = [
        pltpu.make_async_remote_copy(
            src_ref=x_ref, dst_ref=x_buf.at[t], send_sem=xs_sem.at[k - 1], recv_sem=xr_sem,
            device_id={"tp": lax.rem(t + k, tps)}, device_id_type=MESH,
        )
        for k in range(1, tps)
    ]
    for copy in x_copies:
        copy.start()

    def piece(j, s, q):
        return w_buf.at[j, pl.ds(pl.multiple_of(s * shard + q * quarter, 16), quarter), :]

    mine = y * 2 + c
    other = (1 - y) * 2 + c

    def z_copy(j, s, way):
        ref = piece(j, s, mine)
        return pltpu.make_async_remote_copy(
            src_ref=ref, dst_ref=ref, send_sem=zs_sem.at[way, j, s], recv_sem=zr_sem.at[j, s],
            device_id={"fsdp": z + 1 if way == 0 else z - 1}, device_id_type=MESH,
        )

    def y_copy(j, s):
        ref = piece(j, s, mine)
        return pltpu.make_async_remote_copy(
            src_ref=ref, dst_ref=ref, send_sem=ys_sem.at[j], recv_sem=yr_sem.at[j, s],
            device_id={"groups": 1 - y}, device_id_type=MESH,
        )

    def c_copy(j, s, q):
        ref = piece(j, s, q)
        return pltpu.make_async_remote_copy(
            src_ref=ref, dst_ref=ref, send_sem=cs_sem.at[j], recv_sem=cr_sem.at[j],
            device_id={"seq": 1 - c}, device_id_type=MESH,
        )

    for j in range(chunks):
        for copy in own_copies[j]:
            copy.wait()

        @pl.when(z + 1 < n)
        def _():
            z_copy(j, z, 0).start()

        @pl.when(z >= 1)
        def _():
            z_copy(j, z, 1).start()

    def z_arrival(j, s, way, go_on):
        ref = piece(j, s, mine)
        pltpu.make_async_copy(ref, ref, zr_sem.at[j, s]).wait()

        @pl.when(go_on)
        def _():
            z_copy(j, s, way).start()

        y_copy(j, s).start()
        c_copy(j, s, mine).start()

    def y_arrival(j, s):
        ref = piece(j, s, other)
        pltpu.make_async_copy(ref, ref, yr_sem.at[j, s]).wait()
        c_copy(j, s, other).start()

    def z_step(j, step):
        @pl.when(z - step >= 0)
        def _():
            z_arrival(j, z - step, 0, z + 1 < n)

        @pl.when(z + step < n)
        def _():
            z_arrival(j, z + step, 1, z >= 1)

    def y_step(j, step):
        @pl.when(z - step >= 0)
        def _():
            y_arrival(j, z - step)

        @pl.when(z + step < n)
        def _():
            y_arrival(j, z + step)

    def weights(j):
        z_step(j, 1)
        if j > 0:
            y_step(j - 1, n - 1)

        @pl.loop(2, n)
        def _(step):
            z_step(j, step)
            y_step(j, step - 1)

    def normalise():
        x_local.wait()
        for copy in x_copies:
            copy.wait_send()
        arrived = x_buf.at[pl.ds(0, tps - 1)]
        pltpu.make_async_copy(arrived, arrived, xr_sem).wait()

        @pl.loop(0, rows // 32)
        def _(i):
            r = pl.ds(pl.multiple_of(i * 32, 32), 32)
            total = jnp.zeros((32, 1), jnp.float32)
            for k in range(tps):
                part = x_buf[k, r, :].astype(jnp.float32)
                total = total + jnp.sum(part * part, axis=-1, keepdims=True)
            scale = lax.rsqrt(total * (1.0 / depth) + EPS)
            for k in range(tps):
                part = x_buf[k, r, :].astype(jnp.float32)
                gain = ngain_ref[:, k * feat:(k + 1) * feat]
                x_buf[k, r, :] = (part * scale * gain).astype(jnp.bfloat16)

    def head_out(values, gain, r, scale):
        values = values * lax.rsqrt(jnp.mean(values * values, axis=-1, keepdims=True) + EPS) * gain
        values = values * cos_ref[r, :] + pltpu.roll(values, HEAD_DIM // 2, 1) * sin_ref[r, :]
        if scale is not None:
            values = values * scale
        return values.astype(jnp.bfloat16)

    def project(j):
        @pl.loop(0, rows // ROWS)
        def _(i):
            r = pl.ds(pl.multiple_of(i * ROWS, ROWS), ROWS)
            total = None
            for k in range(tps):
                part = jnp.dot(
                    x_buf[k, r, :], w_buf[j, k * feat:(k + 1) * feat, :], preferred_element_type=jnp.float32
                )
                total = part if total is None else total + part
            for h in range(width // HEAD_DIM):
                cols = slice(h * HEAD_DIM, (h + 1) * HEAD_DIM)
                values = total[:, cols]
                if j > 0:
                    done = head_out(values, qgain_ref[...], r, HEAD_DIM ** (-0.5))
                elif h * HEAD_DIM < half:
                    done = head_out(values, kgain_ref[...], r, None)
                else:
                    done = values.astype(jnp.bfloat16)
                s_buf[j, r, cols] = done

    def slab_of(p):
        return pl.ds(pl.multiple_of(p * slab, 16), slab)

    def dispatch_local(j):
        return pltpu.make_async_copy(s_buf.at[j, slab_of(me), :], r_buf.at[j, slab_of(me), :], dl_sem.at[j])

    def dispatch(j):
        @pl.loop(1, peers)
        def _(k):
            p, dev = peer_of(k)
            pltpu.make_async_remote_copy(
                src_ref=s_buf.at[j, slab_of(p), :], dst_ref=r_buf.at[j, slab_of(me), :],
                send_sem=ds_sem.at[j], recv_sem=dr_sem.at[j], device_id=dev, device_id_type=MESH,
            ).start()

        dispatch_local(j).start()

    def dispatched(j):
        dispatch_local(j).wait()
        ref = r_buf.at[j, pl.ds(0, (peers - 1) * slab), :]
        pltpu.make_async_copy(ref, ref, dr_sem.at[j]).wait()

    def attend(j):
        kv = ((j - 1) * width) // (GROUP * HEAD_DIM)

        @pl.loop(0, rows // ROWS)
        def _(i):
            r = pl.ds(pl.multiple_of(i * ROWS, ROWS), ROWS)
            key = r_buf[0, :, kv * HEAD_DIM:(kv + 1) * HEAD_DIM]
            value = r_buf[0, :, half + kv * HEAD_DIM:half + (kv + 1) * HEAD_DIM]
            for h in range(width // HEAD_DIM):
                cols = slice(h * HEAD_DIM, (h + 1) * HEAD_DIM)
                scores = lax.dot_general(
                    r_buf[j, r, cols], key, (((1,), (1,)), ((), ())), preferred_element_type=jnp.float32
                )
                scores = scores + bias_ref[r, :].astype(jnp.float32)
                exponent = jnp.exp(scores - jnp.max(scores, axis=1, keepdims=True))
                total = jnp.sum(exponent, axis=1, keepdims=True)
                out = jnp.dot(exponent.astype(jnp.bfloat16), value, preferred_element_type=jnp.float32)
                o_buf[j - 1, r, cols] = (out / total).astype(jnp.bfloat16)

    def back_local(j):
        return pltpu.make_async_copy(
            o_buf.at[j - 1, slab_of(me), :], ret_ref.at[slab_of(me), pl.ds((j - 1) * width, width)], bl_sem.at[j - 1]
        )

    def back(j):
        @pl.loop(1, peers)
        def _(k):
            p, dev = peer_of(k)
            pltpu.make_async_remote_copy(
                src_ref=o_buf.at[j - 1, slab_of(p), :],
                dst_ref=ret_ref.at[slab_of(me), pl.ds((j - 1) * width, width)],
                send_sem=bs_sem.at[j - 1], recv_sem=br_sem.at[j - 1], device_id=dev, device_id_type=MESH,
            ).start()

        back_local(j).start()

    def ready(j):
        ref = w_buf.at[j, pl.ds(0, 2 * (n - 1) * quarter), :]
        pltpu.make_async_copy(ref, ref, cr_sem.at[j]).wait()

    def serve(j):
        if j == 1:
            dispatched(0)
        dispatched(j)
        attend(j)
        back(j)

    for j in range(chunks + 1):
        if j < chunks:
            weights(j)
        else:
            y_step(chunks - 1, n - 1)
        if j == 1:
            normalise()
        if j >= 1:
            ready(j - 1)
            project(j - 1)
            dispatch(j - 1)
        if j >= 4:
            serve(j - 3)
    for j in range(chunks - 2, chunks):
        serve(j)

    for j in range(1, chunks):
        back_local(j).wait()
        ref = ret_ref.at[pl.ds(0, (peers - 1) * slab), pl.ds((j - 1) * width, width)]
        pltpu.make_async_copy(ref, ref, br_sem.at[j - 1]).wait()
        ref = o_buf.at[j - 1, pl.ds(0, (peers - 1) * slab), :]
        pltpu.make_async_copy(ref, ref, bs_sem.at[j - 1]).wait()
    for j in range(chunks):
        ref = s_buf.at[j, pl.ds(0, (peers - 1) * slab), :]
        pltpu.make_async_copy(ref, ref, ds_sem.at[j]).wait()
        ref = w_buf.at[j, pl.ds(0, (n - 1) * quarter), :]
        pltpu.make_async_copy(ref, ref, ys_sem.at[j]).wait()
        ref = w_buf.at[j, pl.ds(0, 2 * (n - 1) * quarter), :]
        pltpu.make_async_copy(ref, ref, cs_sem.at[j]).wait()

        @pl.loop(0, n)
        def _(s):
            ref = piece(j, s, mine)

            @pl.when((s <= z) & (z + 1 < n))
            def _():
                pltpu.make_async_copy(ref, ref, zs_sem.at[0, j, s]).wait()

            @pl.when((s >= z) & (z >= 1))
            def _():
                pltpu.make_async_copy(ref, ref, zs_sem.at[1, j, s]).wait()


def body(tokens, doc_ids, block_dest, norm_gain, w_query, w_key, w_value, query_gain, key_gain):
    n = lax.axis_size("fsdp")
    tps = lax.axis_size("tp")
    cores = lax.axis_size("seq")
    peers = n * cores
    row_count, feat = tokens.shape
    block_count = row_count // BLOCK
    room = (block_count + peers - 1) // peers
    spots = peers * room
    rows = spots * BLOCK
    width = 2 * w_key.shape[1]
    query_cols = w_query.shape[1]
    nq = query_cols // width
    chunks = nq + 1
    depth = w_key.shape[0] * n

    target = block_dest // block_count
    slot = block_dest % block_count
    onehot = (target[:, None] == jnp.arange(peers, dtype=jnp.int32)[None, :]).astype(jnp.int32)
    before = jnp.cumsum(onehot, axis=0) - onehot
    place = target * room + jnp.sum(before * onehot, axis=1)
    spot = jnp.arange(spots, dtype=jnp.int32)
    match = (place[None, :] == spot[:, None]).astype(jnp.int32)
    filled = jnp.sum(match, axis=1)
    picked = jnp.sum(match * jnp.arange(block_count, dtype=jnp.int32)[None, :], axis=1)
    labels = jnp.sum(match * slot[None, :], axis=1) + (filled - 1)
    packed = tokens.reshape(block_count, BLOCK, feat)[picked].reshape(rows, feat)

    row_index = jnp.arange(row_count, dtype=jnp.int32)
    first = jnp.sum((doc_ids[None, :] < doc_ids[:, None]).astype(jnp.int32), axis=1)
    position = row_index - first
    notes = jnp.concatenate(
        [jnp.broadcast_to(position[None, :], (peers, row_count)), labels.reshape(peers, room)], axis=1
    )
    notes = lax.all_to_all(notes, ("fsdp", "seq"), split_axis=0, concat_axis=0, tiled=True)
    positions = notes[:, :row_count].reshape(peers, block_count, BLOCK)
    tags = notes[:, row_count:].reshape(spots)
    hit = (labels.reshape(peers, room)[:, :, None] == jnp.arange(block_count, dtype=jnp.int32)).astype(jnp.int32)
    packed_position = jnp.sum(hit[:, :, :, None] * positions[:, None, :, :], axis=2).reshape(rows)
    frequency = THETA ** (-jnp.arange(HEAD_DIM // 2, dtype=jnp.float32) * 2.0 / HEAD_DIM)
    angles = packed_position.astype(jnp.float32)[:, None] * frequency[None, :]
    cosine, sine = jnp.cos(angles), jnp.sin(angles)
    cosine = jnp.concatenate([cosine, cosine], axis=1)
    sine = jnp.concatenate([-sine, sine], axis=1)
    seat = (tags[:, None] == jnp.arange(block_count, dtype=jnp.int32)[None, :]).astype(jnp.int32)
    docs = jnp.sum(seat[:, :, None] * (doc_ids.reshape(block_count, BLOCK) + 1)[None], axis=1).reshape(rows)
    order = (tags[:, None] * BLOCK + jnp.arange(BLOCK, dtype=jnp.int32)[None, :]).reshape(rows)
    allowed = (docs[:, None] == docs[None, :]) & (order[None, :] <= order[:, None])
    bias = jnp.where(allowed, 0.0, -1e30).astype(jnp.bfloat16)

    hbm = pl.BlockSpec(memory_space=pl.ANY)
    vmem = pl.BlockSpec(memory_space=pltpu.VMEM)
    dma = pltpu.SemaphoreType.DMA
    returned = pl.pallas_call(
        functools.partial(kernel, (n, tps, cores)),
        out_shape=jax.ShapeDtypeStruct((rows, query_cols), jnp.bfloat16),
        in_specs=[hbm] * 4 + [vmem] * 6,
        out_specs=hbm,
        scratch_shapes=[
            pltpu.VMEM((chunks, depth, width), jnp.bfloat16),
            pltpu.VMEM((tps, rows, feat), jnp.bfloat16),
            pltpu.VMEM((chunks, rows, width), jnp.bfloat16),
            pltpu.VMEM((chunks, rows, width), jnp.bfloat16),
            pltpu.VMEM((nq, rows, width), jnp.bfloat16),
            dma((chunks + 1,)), dma, dma((tps - 1,)), dma,
            dma((2, chunks, n)), dma((chunks, n)),
            dma((chunks,)), dma((chunks, n)),
            dma((chunks,)), dma((chunks,)),
            dma((chunks,)), dma((chunks,)), dma((chunks,)),
            dma((nq,)), dma((nq,)), dma((nq,)),
        ],
        compiler_params=pltpu.CompilerParams(
            collective_id=0, has_side_effects=True, vmem_limit_bytes=62 * 1024 * 1024
        ),
        cost_estimate=pl.CostEstimate(
            flops=2 * rows * depth * width * chunks + 4 * rows * rows * query_cols,
            bytes_accessed=2 * depth * width * chunks, transcendentals=rows * rows * query_cols // HEAD_DIM,
        ),
    )(
        packed, w_query, w_key, w_value, norm_gain[None, :], query_gain[None, :], key_gain[None, :],
        cosine, sine, bias,
    )
    return returned.reshape(spots, BLOCK, query_cols)[place].reshape(row_count, query_cols)


def solution(mesh):
    in_specs = (
        P(("groups", "fsdp", "seq"), "tp"),
        P(("groups", "fsdp", "seq")),
        P(("groups", "fsdp", "seq")),
        P(),
        P("fsdp", "tp"),
        P("fsdp", "tp"),
        P("fsdp", "tp"),
        P(),
        P(),
    )
    out_specs = P(("groups", "fsdp", "seq"), "tp")
    return jax.shard_map(body, mesh=mesh, in_specs=in_specs, out_specs=out_specs, check_vma=False)
```

```python
import functools

import jax
import jax.numpy as jnp
from jax import lax
from jax.experimental import pallas as pl
from jax.experimental.pallas import tpu as pltpu
from jax.sharding import PartitionSpec as P

HEAD_DIM = 128
BLOCK = 16
GROUP = 8
ROWS = 256
EPS = 1e-06
THETA = 1000000.0
MESH = pl.DeviceIdType.MESH


def kernel(
    sizes, x_ref, wq_ref, wk_ref, wv_ref, ngain_ref, qgain_ref, kgain_ref, cos_ref, sin_ref, bias_ref,
    ret_ref, w_buf, x_buf, s_buf, r_buf, o_buf,
    own_sem, xl_sem, xs_sem, xr_sem, zs_sem, zr_sem, ys_sem, yr_sem, cs_sem, cr_sem,
    dl_sem, ds_sem, dr_sem, bl_sem, bs_sem, br_sem,
):
    n, tps, cores = sizes
    y, z, t, c = (lax.axis_index(a) for a in ("groups", "fsdp", "tp", "seq"))
    chunks, depth, width = w_buf.shape
    shard = depth // n
    quarter = shard // 4
    rows = x_ref.shape[0]
    feat = x_ref.shape[1]
    peers = n * cores
    slab = rows // peers
    half = width // 2
    me = z * cores + c

    own_rows = pl.ds(pl.multiple_of(z * shard, 16), shard)
    own_copies = [
        [
            pltpu.make_async_copy(wk_ref, w_buf.at[0, own_rows, pl.ds(0, half)], own_sem.at[0]),
            pltpu.make_async_copy(wv_ref, w_buf.at[0, own_rows, pl.ds(half, half)], own_sem.at[chunks]),
        ]
    ]
    for j in range(1, chunks):
        own_copies.append(
            [pltpu.make_async_copy(wq_ref.at[:, pl.ds((j - 1) * width, width)], w_buf.at[j, own_rows, :], own_sem.at[j])]
        )
    for copies in own_copies:
        for copy in copies:
            copy.start()
    x_local = pltpu.make_async_copy(x_ref, x_buf.at[t], xl_sem)
    x_local.start()

    barrier = pltpu.get_barrier_semaphore()

    def peer_of(k):
        p = lax.rem(me + k, peers)
        return p, {"fsdp": p // cores, "seq": lax.rem(p, cores)}

    @pl.loop(1, peers)
    def _(k):
        _, dev = peer_of(k)
        pl.semaphore_signal(barrier, inc=1, device_id=dev, device_id_type=MESH)

    for k in range(1, tps):
        pl.semaphore_signal(barrier, inc=1, device_id={"tp": lax.rem(t + k, tps)}, device_id_type=MESH)
    pl.semaphore_signal(barrier, inc=1, device_id={"groups": 1 - y}, device_id_type=MESH)
    pl.semaphore_wait(barrier, peers - 1 + tps - 1 + 1)

    x_copies = [
        pltpu.make_async_remote_copy(
            src_ref=x_ref, dst_ref=x_buf.at[t], send_sem=xs_sem.at[k - 1], recv_sem=xr_sem,
            device_id={"tp": lax.rem(t + k, tps)}, device_id_type=MESH,
        )
        for k in range(1, tps)
    ]
    for copy in x_copies:
        copy.start()

    def piece(j, s, q):
        return w_buf.at[j, pl.ds(pl.multiple_of(s * shard + q * quarter, 16), quarter), :]

    mine = y * 2 + c
    other = (1 - y) * 2 + c

    def z_copy(j, s, way):
        ref = piece(j, s, mine)
        return pltpu.make_async_remote_copy(
            src_ref=ref, dst_ref=ref, send_sem=zs_sem.at[way, j, s], recv_sem=zr_sem.at[j, s],
            device_id={"fsdp": z + 1 if way == 0 else z - 1}, device_id_type=MESH,
        )

    def y_copy(j, s):
        ref = piece(j, s, mine)
        return pltpu.make_async_remote_copy(
            src_ref=ref, dst_ref=ref, send_sem=ys_sem.at[j], recv_sem=yr_sem.at[j, s],
            device_id={"groups": 1 - y}, device_id_type=MESH,
        )

    def c_copy(j, s, q):
        ref = piece(j, s, q)
        return pltpu.make_async_remote_copy(
            src_ref=ref, dst_ref=ref, send_sem=cs_sem.at[j], recv_sem=cr_sem.at[j],
            device_id={"seq": 1 - c}, device_id_type=MESH,
        )

    for j in range(chunks):
        for copy in own_copies[j]:
            copy.wait()

        @pl.when(z + 1 < n)
        def _():
            z_copy(j, z, 0).start()

        @pl.when(z >= 1)
        def _():
            z_copy(j, z, 1).start()

    def z_arrival(j, s, way, go_on):
        ref = piece(j, s, mine)
        pltpu.make_async_copy(ref, ref, zr_sem.at[j, s]).wait()

        @pl.when(go_on)
        def _():
            z_copy(j, s, way).start()

        y_copy(j, s).start()
        c_copy(j, s, mine).start()

    def y_arrival(j, s):
        ref = piece(j, s, other)
        pltpu.make_async_copy(ref, ref, yr_sem.at[j, s]).wait()
        c_copy(j, s, other).start()

    def z_step(j, step):
        @pl.when(z - step >= 0)
        def _():
            z_arrival(j, z - step, 0, z + 1 < n)

        @pl.when(z + step < n)
        def _():
            z_arrival(j, z + step, 1, z >= 1)

    def y_step(j, step):
        @pl.when(z - step >= 0)
        def _():
            y_arrival(j, z - step)

        @pl.when(z + step < n)
        def _():
            y_arrival(j, z + step)

    def weights(j):
        @pl.loop(1, n)
        def _(step):
            z_step(j, step)
            if j > 0:
                y_step(j - 1, step)

    def normalise():
        x_local.wait()
        for copy in x_copies:
            copy.wait_send()
        arrived = x_buf.at[pl.ds(0, tps - 1)]
        pltpu.make_async_copy(arrived, arrived, xr_sem).wait()

        @pl.loop(0, rows // 32)
        def _(i):
            r = pl.ds(pl.multiple_of(i * 32, 32), 32)
            total = jnp.zeros((32, 1), jnp.float32)
            for k in range(tps):
                part = x_buf[k, r, :].astype(jnp.float32)
                total = total + jnp.sum(part * part, axis=-1, keepdims=True)
            scale = lax.rsqrt(total * (1.0 / depth) + EPS)
            for k in range(tps):
                part = x_buf[k, r, :].astype(jnp.float32)
                gain = ngain_ref[:, k * feat:(k + 1) * feat]
                x_buf[k, r, :] = (part * scale * gain).astype(jnp.bfloat16)

    def head_out(values, gain, r, scale):
        values = values * lax.rsqrt(jnp.mean(values * values, axis=-1, keepdims=True) + EPS) * gain
        values = values * cos_ref[r, :] + pltpu.roll(values, HEAD_DIM // 2, 1) * sin_ref[r, :]
        if scale is not None:
            values = values * scale
        return values.astype(jnp.bfloat16)

    def project(j):
        @pl.loop(0, rows // ROWS)
        def _(i):
            r = pl.ds(pl.multiple_of(i * ROWS, ROWS), ROWS)
            total = None
            for k in range(tps):
                part = jnp.dot(
                    x_buf[k, r, :], w_buf[j, k * feat:(k + 1) * feat, :], preferred_element_type=jnp.float32
                )
                total = part if total is None else total + part
            for h in range(width // HEAD_DIM):
                cols = slice(h * HEAD_DIM, (h + 1) * HEAD_DIM)
                values = total[:, cols]
                if j > 0:
                    done = head_out(values, qgain_ref[...], r, HEAD_DIM ** (-0.5))
                elif h * HEAD_DIM < half:
                    done = head_out(values, kgain_ref[...], r, None)
                else:
                    done = values.astype(jnp.bfloat16)
                s_buf[j, r, cols] = done

    def slab_of(p):
        return pl.ds(pl.multiple_of(p * slab, 16), slab)

    def dispatch_local(j):
        return pltpu.make_async_copy(s_buf.at[j, slab_of(me), :], r_buf.at[j, slab_of(me), :], dl_sem.at[j])

    def dispatch(j):
        @pl.loop(1, peers)
        def _(k):
            p, dev = peer_of(k)
            pltpu.make_async_remote_copy(
                src_ref=s_buf.at[j, slab_of(p), :], dst_ref=r_buf.at[j, slab_of(me), :],
                send_sem=ds_sem.at[j], recv_sem=dr_sem.at[j], device_id=dev, device_id_type=MESH,
            ).start()

        dispatch_local(j).start()

    def dispatched(j):
        dispatch_local(j).wait()
        ref = r_buf.at[j, pl.ds(0, (peers - 1) * slab), :]
        pltpu.make_async_copy(ref, ref, dr_sem.at[j]).wait()

    def attend(j):
        kv = ((j - 1) * width) // (GROUP * HEAD_DIM)

        @pl.loop(0, rows // ROWS)
        def _(i):
            r = pl.ds(pl.multiple_of(i * ROWS, ROWS), ROWS)
            key = r_buf[0, :, kv * HEAD_DIM:(kv + 1) * HEAD_DIM]
            value = r_buf[0, :, half + kv * HEAD_DIM:half + (kv + 1) * HEAD_DIM]
            for h in range(width // HEAD_DIM):
                cols = slice(h * HEAD_DIM, (h + 1) * HEAD_DIM)
                scores = lax.dot_general(
                    r_buf[j, r, cols], key, (((1,), (1,)), ((), ())), preferred_element_type=jnp.float32
                )
                scores = scores + bias_ref[r, :].astype(jnp.float32)
                exponent = jnp.exp(scores - jnp.max(scores, axis=1, keepdims=True))
                total = jnp.sum(exponent, axis=1, keepdims=True)
                out = jnp.dot(exponent.astype(jnp.bfloat16), value, preferred_element_type=jnp.float32)
                o_buf[j - 1, r, cols] = (out / total).astype(jnp.bfloat16)

    def back_local(j):
        return pltpu.make_async_copy(
            o_buf.at[j - 1, slab_of(me), :], ret_ref.at[slab_of(me), pl.ds((j - 1) * width, width)], bl_sem.at[j - 1]
        )

    def back(j):
        @pl.loop(1, peers)
        def _(k):
            p, dev = peer_of(k)
            pltpu.make_async_remote_copy(
                src_ref=o_buf.at[j - 1, slab_of(p), :],
                dst_ref=ret_ref.at[slab_of(me), pl.ds((j - 1) * width, width)],
                send_sem=bs_sem.at[j - 1], recv_sem=br_sem.at[j - 1], device_id=dev, device_id_type=MESH,
            ).start()

        back_local(j).start()

    def ready(j):
        ref = w_buf.at[j, pl.ds(0, 2 * (n - 1) * quarter), :]
        pltpu.make_async_copy(ref, ref, cr_sem.at[j]).wait()

    def serve(j):
        if j == 1:
            dispatched(0)
        dispatched(j)
        attend(j)
        back(j)

    for j in range(chunks + 1):
        if j < chunks:
            weights(j)
        else:
            @pl.loop(1, n)
            def _(step):
                y_step(chunks - 1, step)
        if j == 3:
            normalise()
        if j >= 3:
            for k in range(0 if j == 3 else j - 1, j):
                ready(k)
                project(k)
                dispatch(k)
        if j >= 4:
            serve(j - 3)
    for j in range(chunks - 2, chunks):
        serve(j)

    for j in range(1, chunks):
        back_local(j).wait()
        ref = ret_ref.at[pl.ds(0, (peers - 1) * slab), pl.ds((j - 1) * width, width)]
        pltpu.make_async_copy(ref, ref, br_sem.at[j - 1]).wait()
        ref = o_buf.at[j - 1, pl.ds(0, (peers - 1) * slab), :]
        pltpu.make_async_copy(ref, ref, bs_sem.at[j - 1]).wait()
    for j in range(chunks):
        ref = s_buf.at[j, pl.ds(0, (peers - 1) * slab), :]
        pltpu.make_async_copy(ref, ref, ds_sem.at[j]).wait()
        ref = w_buf.at[j, pl.ds(0, (n - 1) * quarter), :]
        pltpu.make_async_copy(ref, ref, ys_sem.at[j]).wait()
        ref = w_buf.at[j, pl.ds(0, 2 * (n - 1) * quarter), :]
        pltpu.make_async_copy(ref, ref, cs_sem.at[j]).wait()

        @pl.loop(0, n)
        def _(s):
            ref = piece(j, s, mine)

            @pl.when((s <= z) & (z + 1 < n))
            def _():
                pltpu.make_async_copy(ref, ref, zs_sem.at[0, j, s]).wait()

            @pl.when((s >= z) & (z >= 1))
            def _():
                pltpu.make_async_copy(ref, ref, zs_sem.at[1, j, s]).wait()


def body(tokens, doc_ids, block_dest, norm_gain, w_query, w_key, w_value, query_gain, key_gain):
    n = lax.axis_size("fsdp")
    tps = lax.axis_size("tp")
    cores = lax.axis_size("seq")
    peers = n * cores
    row_count, feat = tokens.shape
    block_count = row_count // BLOCK
    room = (block_count + peers - 1) // peers
    spots = peers * room
    rows = spots * BLOCK
    width = 2 * w_key.shape[1]
    query_cols = w_query.shape[1]
    nq = query_cols // width
    chunks = nq + 1
    depth = w_key.shape[0] * n

    target = block_dest // block_count
    slot = block_dest % block_count
    onehot = (target[:, None] == jnp.arange(peers, dtype=jnp.int32)[None, :]).astype(jnp.int32)
    before = jnp.cumsum(onehot, axis=0) - onehot
    place = target * room + jnp.sum(before * onehot, axis=1)
    spot = jnp.arange(spots, dtype=jnp.int32)
    match = (place[None, :] == spot[:, None]).astype(jnp.int32)
    filled = jnp.sum(match, axis=1)
    picked = jnp.sum(match * jnp.arange(block_count, dtype=jnp.int32)[None, :], axis=1)
    labels = jnp.sum(match * slot[None, :], axis=1) + (filled - 1)
    packed = tokens.reshape(block_count, BLOCK, feat)[picked].reshape(rows, feat)

    row_index = jnp.arange(row_count, dtype=jnp.int32)
    first = jnp.sum((doc_ids[None, :] < doc_ids[:, None]).astype(jnp.int32), axis=1)
    position = row_index - first
    notes = jnp.concatenate(
        [jnp.broadcast_to(position[None, :], (peers, row_count)), labels.reshape(peers, room)], axis=1
    )
    notes = lax.all_to_all(notes, ("fsdp", "seq"), split_axis=0, concat_axis=0, tiled=True)
    positions = notes[:, :row_count].reshape(peers, block_count, BLOCK)
    tags = notes[:, row_count:].reshape(spots)
    hit = (labels.reshape(peers, room)[:, :, None] == jnp.arange(block_count, dtype=jnp.int32)).astype(jnp.int32)
    packed_position = jnp.sum(hit[:, :, :, None] * positions[:, None, :, :], axis=2).reshape(rows)
    frequency = THETA ** (-jnp.arange(HEAD_DIM // 2, dtype=jnp.float32) * 2.0 / HEAD_DIM)
    angles = packed_position.astype(jnp.float32)[:, None] * frequency[None, :]
    cosine, sine = jnp.cos(angles), jnp.sin(angles)
    cosine = jnp.concatenate([cosine, cosine], axis=1)
    sine = jnp.concatenate([-sine, sine], axis=1)
    seat = (tags[:, None] == jnp.arange(block_count, dtype=jnp.int32)[None, :]).astype(jnp.int32)
    docs = jnp.sum(seat[:, :, None] * (doc_ids.reshape(block_count, BLOCK) + 1)[None], axis=1).reshape(rows)
    order = (tags[:, None] * BLOCK + jnp.arange(BLOCK, dtype=jnp.int32)[None, :]).reshape(rows)
    allowed = (docs[:, None] == docs[None, :]) & (order[None, :] <= order[:, None])
    bias = jnp.where(allowed, 0.0, -1e30).astype(jnp.bfloat16)

    hbm = pl.BlockSpec(memory_space=pl.ANY)
    vmem = pl.BlockSpec(memory_space=pltpu.VMEM)
    dma = pltpu.SemaphoreType.DMA
    returned = pl.pallas_call(
        functools.partial(kernel, (n, tps, cores)),
        out_shape=jax.ShapeDtypeStruct((rows, query_cols), jnp.bfloat16),
        in_specs=[hbm] * 4 + [vmem] * 6,
        out_specs=hbm,
        scratch_shapes=[
            pltpu.VMEM((chunks, depth, width), jnp.bfloat16),
            pltpu.VMEM((tps, rows, feat), jnp.bfloat16),
            pltpu.VMEM((chunks, rows, width), jnp.bfloat16),
            pltpu.VMEM((chunks, rows, width), jnp.bfloat16),
            pltpu.VMEM((nq, rows, width), jnp.bfloat16),
            dma((chunks + 1,)), dma, dma((tps - 1,)), dma,
            dma((2, chunks, n)), dma((chunks, n)),
            dma((chunks,)), dma((chunks, n)),
            dma((chunks,)), dma((chunks,)),
            dma((chunks,)), dma((chunks,)), dma((chunks,)),
            dma((nq,)), dma((nq,)), dma((nq,)),
        ],
        compiler_params=pltpu.CompilerParams(
            collective_id=0, has_side_effects=True, vmem_limit_bytes=62 * 1024 * 1024
        ),
        cost_estimate=pl.CostEstimate(
            flops=2 * rows * depth * width * chunks + 4 * rows * rows * query_cols,
            bytes_accessed=2 * depth * width * chunks, transcendentals=rows * rows * query_cols // HEAD_DIM,
        ),
    )(
        packed, w_query, w_key, w_value, norm_gain[None, :], query_gain[None, :], key_gain[None, :],
        cosine, sine, bias,
    )
    return returned.reshape(spots, BLOCK, query_cols)[place].reshape(row_count, query_cols)


def solution(mesh):
    in_specs = (
        P(("groups", "fsdp", "seq"), "tp"),
        P(("groups", "fsdp", "seq")),
        P(("groups", "fsdp", "seq")),
        P(),
        P("fsdp", "tp"),
        P("fsdp", "tp"),
        P("fsdp", "tp"),
        P(),
        P(),
    )
    out_specs = P(("groups", "fsdp", "seq"), "tp")
    return jax.shard_map(body, mesh=mesh, in_specs=in_specs, out_specs=out_specs, check_vma=False)
```
